32 devices in a mesh: dp: 4 (over x, core), fsdp: 8 (over z, y).
Axes of the slice: x: 2, y: 2, z: 4, core: 2. Of those that a mesh axis runs over, the one named last changes fastest.
Arguments:
- attention_input: bfloat16 [8192, 768], P('fsdp', 'dp')
- feedforward_input: bfloat16 [14336, 768], P('fsdp', 'dp')
- attention_cotangent: bfloat16 [8192, 768], P(('dp', 'fsdp'))
- feedforward_cotangent: bfloat16 [8192, 768], P(('dp', 'fsdp'))
- lengths: int32 [12], replicated, may hold values from 16 to 64, as said below
- groups: int32 [12], replicated, may hold values from 0 to 3, as said below
- attention_weight: bfloat16 [8192, 8192], P('fsdp', 'dp'), may hold values from -0.29882812 to 0.29882812
- attention_moment: bfloat16 [8192, 8192], P('fsdp', 'dp'), may hold values from -0.59765625 to 0.59765625
- attention_second: bfloat16 [8192, 8192], P('fsdp', 'dp'), may hold values from 0.0099487305 to 1
- feedforward_weight: bfloat16 [14336, 8192], P('fsdp', 'dp'), may hold values from -0.29882812 to 0.29882812
- feedforward_moment: bfloat16 [14336, 8192], P('fsdp', 'dp'), may hold values from -0.59765625 to 0.59765625
- feedforward_second: bfloat16 [14336, 8192], P('fsdp', 'dp'), may hold values from 0.0099487305 to 1
Outputs:
- new_attention_weight: bfloat16 [8192, 8192], P('fsdp', 'dp')
- new_attention_moment: bfloat16 [8192, 8192], P('fsdp', 'dp')
- new_attention_second: bfloat16 [8192, 8192], P('fsdp', 'dp')
- new_feedforward_weight: bfloat16 [14336, 8192], P('fsdp', 'dp')
- new_feedforward_moment: bfloat16 [14336, 8192], P('fsdp', 'dp')
- new_feedforward_second: bfloat16 [14336, 8192], P('fsdp', 'dp')
The draws below stay inside these ranges and needn't reach their ends.
Inputs may be any that keep to these rules, and one draw needn't show every extreme that they name: `lengths`: some example has exactly 64 live tokens. `groups`: every group has at least one example.
All inputs are finite; a program needn't handle non-finite values.
Results may differ from the reference program's by a relative error of at most 0.0038.
Values may be sent and summed in bfloat16 or wider, within the bound.
A program may use at most 192 MiB of HBM per device.

```python
import math
import jax
import jax.numpy as jnp
from jax import lax

D = 8192
FF_WIN = 14336
SLOT = 64
GROUPS = 4
EXAMPLES = 12
TOKENS = 768


region_count = 8


def scaled_field(key, height, magnitude):
    jitter_key, row_key, region_key = jax.random.split(key, 3)
    jitter = jax.random.normal(jitter_key, (height, TOKENS), jnp.float32)
    row_factor = jnp.exp(jax.random.uniform(row_key, (height, EXAMPLES, 1), jnp.float32, math.log(0.5), math.log(2.0)))
    region_factor = jnp.exp(jax.random.uniform(region_key, (region_count, EXAMPLES, 1), jnp.float32, math.log(0.2), math.log(5.0)))
    region_of_row = jnp.arange(height, dtype=jnp.int32) * region_count // height
    region_rows = region_factor[region_of_row]
    spread = jnp.broadcast_to(row_factor * region_rows, (height, EXAMPLES, SLOT)).reshape(height, TOKENS)
    return magnitude * jitter * spread


def draw_attention_input(key, part):
    return scaled_field(jax.random.fold_in(key, 11), D, 1.0).astype(jnp.bfloat16)


def draw_feedforward_input(key, part):
    return scaled_field(jax.random.fold_in(key, 12), FF_WIN, 1.0).astype(jnp.bfloat16)


def draw_attention_cotangent(key, part):
    return scaled_field(jax.random.fold_in(key, 13), D, 0.05).astype(jnp.bfloat16)


def draw_feedforward_cotangent(key, part):
    return scaled_field(jax.random.fold_in(key, 14), D, 0.05).astype(jnp.bfloat16)


def draw_lengths(key, part):
    values_key, marked_key = jax.random.split(jax.random.fold_in(key, 21))
    values = jax.random.randint(values_key, (EXAMPLES,), max(SLOT // 4, 1), SLOT + 1)
    marked = jax.random.randint(marked_key, (), 0, EXAMPLES)
    return jnp.where(jnp.arange(EXAMPLES) == marked, SLOT, values).astype(jnp.int32)


def draw_groups(key, part):
    values_key, shuffle_key = jax.random.split(jax.random.fold_in(key, 22))
    values = jax.random.randint(values_key, (EXAMPLES,), 0, GROUPS)
    shuffled = jax.random.permutation(shuffle_key, EXAMPLES)
    return values.at[shuffled[:GROUPS]].set(jnp.arange(GROUPS, dtype=jnp.int32)).astype(jnp.int32)


def level_of(key, extent, pieces, smallest, largest):
    level = 1.0
    for dim, blocks in pieces:
        heights = jax.random.uniform(jax.random.fold_in(jax.random.fold_in(key, 6), dim), (blocks,), jnp.float32, smallest / len(pieces), largest / len(pieces))
        level = level * jnp.repeat(jnp.exp(heights), extent[dim] // blocks).reshape((-1,) + (1,) * (len(extent) - 1 - dim))
    return level


def scatter_about(stream_key, extent, deviation, reach, shards=(), kind=jnp.bfloat16):
    entries = jax.random.normal(stream_key, extent, jnp.float32) * deviation
    if len(shards) > 0:
        entries = level_of(stream_key, extent, shards, -0.22, 0.18) * entries
    return jnp.clip(entries, min=-reach, max=reach).astype(kind)


def setup_inputs(seed: int = 0) -> dict:
    seeds = jax.random.split(jax.random.key(seed), 13)
    return {
        "attention_input": draw_attention_input(jax.random.fold_in(seeds[12], 71), 0),
        "feedforward_input": draw_feedforward_input(jax.random.fold_in(seeds[12], 71), 0),
        "attention_cotangent": draw_attention_cotangent(jax.random.fold_in(seeds[12], 71), 0),
        "feedforward_cotangent": draw_feedforward_cotangent(jax.random.fold_in(seeds[12], 71), 0),
        "lengths": draw_lengths(jax.random.fold_in(seeds[12], 71), 0),
        "groups": draw_groups(jax.random.fold_in(seeds[12], 71), 0),
        "attention_weight": scatter_about(seeds[6], (D, D), 0.05, 0.29882812, ((0, 8), (1, 4))),
        "attention_moment": scatter_about(seeds[7], (D, D), 0.1, 0.59765625, ((0, 8), (1, 4))),
        "attention_second": jnp.clip(jnp.exp(math.log(1.0) - 4.61031033 * jax.random.uniform(seeds[8], (D, D), jnp.float32) ** level_of(seeds[8], (D, D), ((0, 8), (1, 4)), -0.2, 0.2)), 0.0099487305, 1.0).astype(jnp.bfloat16),
        "feedforward_weight": scatter_about(seeds[9], (FF_WIN, D), 0.05, 0.29882812, ((0, 8), (1, 4))),
        "feedforward_moment": scatter_about(seeds[10], (FF_WIN, D), 0.1, 0.59765625, ((0, 8), (1, 4))),
        "feedforward_second": jnp.clip(jnp.exp(math.log(1.0) - 4.61031033 * jax.random.uniform(seeds[11], (FF_WIN, D), jnp.float32) ** level_of(seeds[11], (FF_WIN, D), ((0, 8), (1, 4)), -0.2, 0.2)), 0.0099487305, 1.0).astype(jnp.bfloat16),
    }


first_decay = 0.9
second_decay = 0.95
first_bias = 1.0 - 0.9 ** 10
second_bias = 1.0 - 0.95 ** 10
learn_rate = 0.01
weight_decay = 0.1
epsilon = 1e-08
norm_epsilon = 1e-06

def live_tokens(lengths, slot_len):
    position = lax.broadcasted_iota(jnp.int32, (lengths.shape[0], slot_len), 1)
    return (position < lengths[:, None]).reshape(-1)

def example_norms(inputs, cotangents, second, slot_len):
    precond = 1.0 / (jnp.sqrt(second.astype(jnp.float32)) + epsilon)
    inputs_wide = inputs.astype(jnp.float32)
    cotangents_wide = cotangents.astype(jnp.float32)
    example_count = inputs.shape[1] // slot_len

    def one_example(example, norm_vals):
        inputs_slot = lax.dynamic_slice_in_dim(inputs_wide, example * slot_len, slot_len, 1)
        grads_slot = lax.dynamic_slice_in_dim(cotangents_wide, example * slot_len, slot_len, 1)
        tile_block = lax.dot_general(inputs_slot, grads_slot, (((1,), (1,)), ((), ())), preferred_element_type=jnp.float32)
        return norm_vals.at[example].set(jnp.sum(tile_block * tile_block * precond))
    return lax.fori_loop(0, example_count, one_example, jnp.zeros((example_count,), jnp.float32))

def importance(norm_vals, groups):
    strength = jnp.sqrt(norm_vals + norm_epsilon)
    same_group = (groups[:, None] == groups[None, :]).astype(jnp.float32)
    group_total = lax.optimization_barrier(jnp.sum(same_group * strength[None, :], axis=1))
    group_count = lax.optimization_barrier(jnp.sum(same_group, axis=1))
    return group_count * strength / group_total

def weighted_gradient(inputs, cotangents, token_weight, example_count):
    scaled = (inputs.astype(jnp.float32) * token_weight[None, :]).astype(jnp.bfloat16)
    product = lax.dot_general(scaled.astype(jnp.float32), cotangents.astype(jnp.float32), (((1,), (1,)), ((), ())), preferred_element_type=jnp.float32)
    return product / example_count

def adamw_step(weight, moment, second, gradient):
    moment_new = first_decay * moment.astype(jnp.float32) + (1.0 - first_decay) * gradient
    second_new = second_decay * second.astype(jnp.float32) + (1.0 - second_decay) * gradient * gradient
    step_dir = moment_new / first_bias / (jnp.sqrt(second_new / second_bias) + epsilon)
    weight_wide = weight.astype(jnp.float32)
    updated = weight_wide - learn_rate * (step_dir + weight_decay * weight_wide)
    return (updated.astype(jnp.bfloat16), moment_new.astype(jnp.bfloat16), second_new.astype(jnp.bfloat16))

def reference(attention_input, feedforward_input, attention_cotangent, feedforward_cotangent, lengths, groups, attention_weight, attention_moment, attention_second, feedforward_weight, feedforward_moment, feedforward_second):
    example_count = lengths.shape[0]
    slot_len = attention_input.shape[1] // example_count
    live_mask = live_tokens(lengths, slot_len)
    attention_live = jnp.where(live_mask[None, :], attention_input, jnp.zeros_like(attention_input))
    feedforward_live = jnp.where(live_mask[None, :], feedforward_input, jnp.zeros_like(feedforward_input))
    norm_vals = example_norms(attention_live, attention_cotangent, attention_second, slot_len) + example_norms(feedforward_live, feedforward_cotangent, feedforward_second, slot_len)
    weights = importance(norm_vals, groups)
    token_weight = jnp.repeat(weights, slot_len) * live_mask.astype(jnp.float32)
    attention_grad = weighted_gradient(attention_live, attention_cotangent, token_weight, example_count)
    feedforward_grad = weighted_gradient(feedforward_live, feedforward_cotangent, token_weight, example_count)
    attention_new = adamw_step(attention_weight, attention_moment, attention_second, attention_grad)
    feedforward_new = adamw_step(feedforward_weight, feedforward_moment, feedforward_second, feedforward_grad)
    return (attention_new[0], attention_new[1], attention_new[2], feedforward_new[0], feedforward_new[1], feedforward_new[2])
```

```python
import functools

import jax
import jax.numpy as jnp
from jax import lax
from jax.experimental import pallas as pl
from jax.experimental.pallas import tpu as pltpu
from jax.sharding import PartitionSpec as P

first_decay = 0.9
second_decay = 0.95
first_bias = 1.0 - 0.9**10
second_bias = 1.0 - 0.95**10
learn_rate = 0.01
weight_decay = 0.1
epsilon = 1e-08
norm_epsilon = 1e-06


def live_tokens(lengths, slot_len):
    position = lax.broadcasted_iota(jnp.int32, (lengths.shape[0], slot_len), 1)
    return (position < lengths[:, None]).reshape(-1)


def example_norms(inputs, cotangents, second, slot_len):
    precond = 1.0 / (jnp.sqrt(second.astype(jnp.float32)) + epsilon)
    example_count = inputs.shape[1] // slot_len

    def one_example(example, norm_vals):
        inputs_slot = lax.dynamic_slice_in_dim(inputs, example * slot_len, slot_len, 1)
        grads_slot = lax.dynamic_slice_in_dim(cotangents, example * slot_len, slot_len, 1)
        tile_block = lax.dot_general(
            inputs_slot, grads_slot, (((1,), (1,)), ((), ())), preferred_element_type=jnp.float32
        )
        return norm_vals.at[example].set(jnp.sum(tile_block * tile_block * precond))

    return lax.fori_loop(0, example_count, one_example, jnp.zeros((example_count,), jnp.float32))


def importance(norm_vals, groups):
    strength = jnp.sqrt(norm_vals + norm_epsilon)
    same_group = (groups[:, None] == groups[None, :]).astype(jnp.float32)
    group_total = jnp.sum(same_group * strength[None, :], axis=1)
    group_count = jnp.sum(same_group, axis=1)
    return group_count * strength / group_total


def weighted_gradient(inputs, cotangents, token_weight, example_count):
    scaled = (inputs.astype(jnp.float32) * token_weight[None, :]).astype(jnp.bfloat16)
    product = lax.dot_general(
        scaled, cotangents, (((1,), (1,)), ((), ())), preferred_element_type=jnp.float32
    )
    return product / example_count


def adamw_step(weight, moment, second, gradient):
    moment_new = first_decay * moment.astype(jnp.float32) + (1.0 - first_decay) * gradient
    second_new = (
        second_decay * second.astype(jnp.float32) + (1.0 - second_decay) * gradient * gradient
    )
    step_dir = moment_new / first_bias / (jnp.sqrt(second_new / second_bias) + epsilon)
    weight_wide = weight.astype(jnp.float32)
    updated = weight_wide - learn_rate * (step_dir + weight_decay * weight_wide)
    return (
        updated.astype(jnp.bfloat16),
        moment_new.astype(jnp.bfloat16),
        second_new.astype(jnp.bfloat16),
    )


def per_device(
    attention_input,
    feedforward_input,
    attention_cotangent,
    feedforward_cotangent,
    lengths,
    groups,
    attention_weight,
    attention_moment,
    attention_second,
    feedforward_weight,
    feedforward_moment,
    feedforward_second,
):
    example_count = lengths.shape[0]
    attention_full, feedforward_full = (
        lax.all_gather(attention_input, "dp", axis=1, tiled=True),
        lax.all_gather(feedforward_input, "dp", axis=1, tiled=True),
    )
    slot_len = attention_full.shape[1] // example_count
    live_mask = live_tokens(lengths, slot_len)
    attention_live = jnp.where(live_mask[None, :], attention_full, jnp.zeros_like(attention_full))
    feedforward_live = jnp.where(
        live_mask[None, :], feedforward_full, jnp.zeros_like(feedforward_full)
    )
    attention_columns, feedforward_columns = (
        lax.all_gather(attention_cotangent, "fsdp", axis=0, tiled=True),
        lax.all_gather(feedforward_cotangent, "fsdp", axis=0, tiled=True),
    )
    attention_part = example_norms(attention_live, attention_columns, attention_second, slot_len)
    feedforward_part = example_norms(
        feedforward_live, feedforward_columns, feedforward_second, slot_len
    )
    norm_vals = lax.psum(attention_part + feedforward_part, ("dp", "fsdp"))
    weights = importance(norm_vals, groups)
    token_weight = jnp.repeat(weights, slot_len) * live_mask.astype(jnp.float32)
    attention_grad = weighted_gradient(
        attention_live, attention_columns, token_weight, example_count
    )
    feedforward_grad = weighted_gradient(
        feedforward_live, feedforward_columns, token_weight, example_count
    )
    attention_new = adamw_step(attention_weight, attention_moment, attention_second, attention_grad)
    feedforward_new = adamw_step(
        feedforward_weight, feedforward_moment, feedforward_second, feedforward_grad
    )
    return (
        attention_new[0],
        attention_new[1],
        attention_new[2],
        feedforward_new[0],
        feedforward_new[1],
        feedforward_new[2],
    )


MESH = pl.DeviceIdType.MESH
TILE = 256
GROUP = 256
ROWS_PAD = 16
VMEM_BYTES = 56 * 2**20


def refined_reciprocal(value):
    guess = pl.reciprocal(value, approx=True)
    return guess * (2.0 - value * guess)


def gather_kernel(
    n, m, slot_len, example_count,
    xa_in, xf_in, ca_in, cf_in, va_in, vf_in, live_ref, same_ref,
    xa_out, xf_out, c_out,
    xa_t, xf_t, x_rows, cbuf, vbuf, acc, norm_f, norm_d,
    local_sem, out_sem, c_send, c_recv, x_send, x_recv, core_send, core_recv,
    f_send, f_recv, d_send, d_recv,
):
    me_d, me_f = lax.axis_index("dp"), lax.axis_index("fsdp")
    position = lax.select(lax.rem(me_f, 2) == 0, me_f // 2, n - 1 - me_f // 2)

    def ring_index(place):
        place = lax.rem(place + n, n)
        return lax.select(place < n // 2, 2 * place, 2 * (n - 1 - place) + 1)

    rows_a, rows_f = xa_in.shape[1], xf_in.shape[1]
    share, block = xa_in.shape[0], ca_in.shape[0]
    tiles_a, tiles_f = rows_a // TILE, rows_f // TILE
    groups = live_ref.shape[1] // GROUP
    per_group = GROUP // slot_len
    high, core, m_high = me_d // 2, lax.rem(me_d, 2), m // 2

    x_bufs = (xa_t, xf_t)

    def x_slot(layer, owner):
        return x_bufs[layer].at[pl.ds(pl.multiple_of(owner * share, 16), share)]

    own = []
    for index, (src, dst) in enumerate((
        (ca_in, cbuf.at[0, me_f]),
        (cf_in, cbuf.at[1, me_f]),
        (xa_in, x_slot(0, me_d)),
        (xf_in, x_slot(1, me_d)),
        (va_in, vbuf.at[pl.ds(0, rows_a)]),
        (vf_in, vbuf.at[pl.ds(rows_a, rows_f)]),
    )):
        copy = pltpu.make_async_copy(src, dst, local_sem.at[index])
        copy.start()
        own.append(copy)

    barrier = pltpu.get_barrier_semaphore()
    for k in range(1, n):
        pl.semaphore_signal(
            barrier, inc=1, device_id={"fsdp": lax.rem(me_f + k, n)}, device_id_type=MESH
        )
    for k in range(1, m):
        pl.semaphore_signal(
            barrier, inc=1, device_id={"dp": lax.rem(me_d + k, m)}, device_id_type=MESH
        )
    pl.semaphore_wait(barrier, n + m - 2)

    def c_copy(layer, way, step):
        sign = 1 - 2 * way
        slot = cbuf.at[layer, ring_index(position - sign * step)]
        return pltpu.make_async_remote_copy(
            src_ref=slot, dst_ref=slot,
            send_sem=c_send.at[layer, way, step], recv_sem=c_recv.at[layer, way, step],
            device_id={"fsdp": ring_index(position + sign)}, device_id_type=MESH,
        )

    def x_copy(layer, k):
        slot = x_slot(layer, me_d)
        return pltpu.make_async_remote_copy(
            src_ref=slot, dst_ref=slot,
            send_sem=x_send.at[layer, k], recv_sem=x_recv.at[layer, k],
            device_id={"dp": lax.rem(high + k, m_high) * 2 + core}, device_id_type=MESH,
        )

    def core_copy(layer, k):
        slot = x_slot(layer, lax.rem(high + m_high - k, m_high) * 2 + core)
        return pltpu.make_async_remote_copy(
            src_ref=slot, dst_ref=slot,
            send_sem=core_send.at[layer, k], recv_sem=core_recv.at[layer, k],
            device_id={"dp": high * 2 + 1 - core}, device_id_type=MESH,
        )

    pairs = [(layer, way) for layer in range(2) for way in range(2)]
    last = n // 2 - 1

    def c_pairs(step):
        return pairs if step < last else [(0, 0), (1, 1)]

    for layer in range(2):
        own[layer].wait()
        for way in range(2):
            c_copy(layer, way, 0).start()
    for layer in range(2):
        own[2 + layer].wait()
        for k in range(1, m_high):
            x_copy(layer, k).start()
        core_copy(layer, 0).start()
    acc[...] = jnp.zeros_like(acc)

    def advance(step):
        for layer, way in c_pairs(step):
            c_copy(layer, way, step).wait_recv()
            if (layer, way) in (c_pairs(step + 1) if step < last else []):
                c_copy(layer, way, step + 1).start()

    def take_inputs(layer):
        for k in range(1, m_high):
            x_copy(layer, k).wait_recv()
            core_copy(layer, k).start()
        for k in range(m_high):
            core_copy(layer, k).wait_recv()
        buf, base, tiles = x_bufs[layer], (0, rows_a)[layer], (tiles_a, tiles_f)[layer]

        def turn(tile, carry):
            here = pl.multiple_of(tile * TILE, TILE)
            there = pl.multiple_of(base + tile * TILE, TILE)
            for g in range(groups):
                x_rows[g, pl.ds(there, TILE), :] = buf[
                    pl.ds(g * GROUP, GROUP), pl.ds(here, TILE)
                ].T
            return carry

        lax.fori_loop(0, tiles, turn, 0)

    def unit(tile_from, tile_to, owner):
        column = pl.multiple_of(owner * block, 128)

        def one_tile(tile, carry):
            layer = lax.select(tile < tiles_a, 0, 1)
            row = pl.multiple_of(tile * TILE, TILE)
            second = vbuf[pl.ds(row, TILE), pl.ds(column, block)].astype(jnp.float32)
            precond = refined_reciprocal(second * lax.rsqrt(second) + epsilon)
            for g in range(groups):
                lhs = x_rows[g, pl.ds(row, TILE), :]
                rhs = cbuf[layer, owner, :, pl.ds(g * GROUP, GROUP)]
                for e in range(g * per_group, (g + 1) * per_group):
                    live = live_ref[pl.ds(e, 1), pl.ds(g * GROUP, GROUP)].astype(jnp.bfloat16)
                    product = lax.dot_general(
                        lhs, rhs * live, (((1,), (1,)), ((), ())),
                        preferred_element_type=jnp.float32,
                    )
                    square = product * product * precond
                    acc[e] += jnp.sum(square.reshape(TILE // 8, 8, block), axis=0)
            return carry

        lax.fori_loop(tile_from, tile_to, one_tile, 0)

    total_tiles = tiles_a + tiles_f

    def both_ways(tile_from, tile_to, step):
        def one_way(way, carry):
            unit(tile_from, tile_to, ring_index(position - (1 - 2 * way) * (step + 1)))
            return carry

        lax.fori_loop(0, 2, one_way, 0)

    own[4].wait()
    own[5].wait()
    take_inputs(0)
    unit(0, tiles_a, me_f)
    advance(0)
    both_ways(0, tiles_a, 0)
    take_inputs(1)
    unit(tiles_a, total_tiles, me_f)
    if last >= 1:
        advance(1)
        if last >= 2:
            both_ways(tiles_a, total_tiles, 0)
    for step in range(2, last + 1):
        advance(step)
        both_ways(0, total_tiles, step - 1)
    unit(0, total_tiles, ring_index(position + n // 2))

    c_store = pltpu.make_async_copy(cbuf, c_out, out_sem)
    c_store.start()

    partial = jnp.sum(jnp.sum(acc[...], axis=1), axis=1, keepdims=True)
    norm_f[me_f] = jnp.broadcast_to(partial, (ROWS_PAD, 128))

    def sum_over(axis, count, me, buf, send, recv):
        copies = []
        for k in range(1, count):
            copy = pltpu.make_async_remote_copy(
                src_ref=buf.at[me], dst_ref=buf.at[me],
                send_sem=send.at[k], recv_sem=recv.at[k],
                device_id={axis: lax.rem(me + k, count)}, device_id_type=MESH,
            )
            copy.start()
            copies.append(copy)
        for copy in copies:
            copy.wait_recv()
        return copies, jnp.sum(buf[...], axis=0)

    f_copies, over_f = sum_over("fsdp", n, me_f, norm_f, f_send, f_recv)
    norm_d[me_d] = over_f
    d_copies, norm_vals = sum_over("dp", m, me_d, norm_d, d_send, d_recv)

    strength = jnp.sqrt(norm_vals + norm_epsilon)
    same = same_ref[...]
    sub = lax.broadcasted_iota(jnp.int32, (ROWS_PAD, 128), 0)
    lane = lax.broadcasted_iota(jnp.int32, (ROWS_PAD, 128), 1)
    strength_row = jnp.sum(jnp.where(sub == lane, strength, 0.0), axis=0, keepdims=True)
    group_total = jnp.sum(same * strength_row, axis=1, keepdims=True)
    group_count = jnp.sum(same, axis=1, keepdims=True)
    weights = group_count * strength[:, :1] / group_total
    token_weight = jnp.sum(live_ref[...] * weights, axis=0, keepdims=True)

    for layer, out in ((0, xa_out), (1, xf_out)):
        base, tiles = (0, rows_a)[layer], (tiles_a, tiles_f)[layer]

        def scale(tile, carry, out=out, base=base):
            here = pl.multiple_of(tile * TILE, TILE)
            there = pl.multiple_of(base + tile * TILE, TILE)
            for g in range(groups):
                lanes = slice(g * GROUP, (g + 1) * GROUP)
                wide = x_rows[g, pl.ds(there, TILE), :].astype(jnp.float32)
                out[pl.ds(here, TILE), lanes] = (wide * token_weight[:, lanes]).astype(jnp.bfloat16)
            return carry

        lax.fori_loop(0, tiles, scale, 0)

    for step in range(last + 1):
        for layer, way in c_pairs(step):
            c_copy(layer, way, step).wait_send()
    for layer in range(2):
        for k in range(1, m_high):
            x_copy(layer, k).wait_send()
        for k in range(m_high):
            core_copy(layer, k).wait_send()
    for copy in f_copies + d_copies:
        copy.wait_send()
    c_store.wait()


def gather_and_weigh(n, m, xa, xf, ca, cf, va, vf, lengths, groups):
    example_count = lengths.shape[0]
    tokens = ca.shape[1]
    slot_len = tokens // example_count
    live = live_tokens(lengths, slot_len)
    example_of = jnp.arange(tokens, dtype=jnp.int32) // slot_len
    row = jnp.arange(ROWS_PAD, dtype=jnp.int32)
    live_hot = ((row[:, None] == example_of[None, :]) & live[None, :]).astype(jnp.float32)
    padded = jnp.concatenate([groups, -1 - jnp.arange(128 - example_count, dtype=jnp.int32)])
    same = (padded[:ROWS_PAD, None] == padded[None, :]).astype(jnp.float32)
    rows_a, rows_f, block = xa.shape[0], xf.shape[0], ca.shape[0]
    columns = n * block
    bf16, f32 = jnp.bfloat16, jnp.float32
    hbm = pl.BlockSpec(memory_space=pl.ANY)
    vmem = pl.BlockSpec(memory_space=pltpu.VMEM)
    dma = pltpu.SemaphoreType.DMA
    return pl.pallas_call(
        functools.partial(gather_kernel, n, m, slot_len, example_count),
        out_shape=(
            jax.ShapeDtypeStruct((rows_a, tokens), bf16),
            jax.ShapeDtypeStruct((rows_f, tokens), bf16),
            jax.ShapeDtypeStruct((2, n, block, tokens), bf16),
        ),
        in_specs=[hbm] * 6 + [vmem] * 2,
        out_specs=(vmem, vmem, hbm),
        scratch_shapes=[
            pltpu.VMEM((tokens, rows_a), bf16),
            pltpu.VMEM((tokens, rows_f), bf16),
            pltpu.VMEM((tokens // GROUP, rows_a + rows_f, GROUP), bf16),
            pltpu.VMEM((2, n, block, tokens), bf16),
            pltpu.VMEM((rows_a + rows_f, columns), bf16),
            pltpu.VMEM((ROWS_PAD, 8, block), f32),
            pltpu.VMEM((n, ROWS_PAD, 128), f32),
            pltpu.VMEM((m, ROWS_PAD, 128), f32),
            dma((6,)),
            dma,
            dma((2, 2, n // 2)),
            dma((2, 2, n // 2)),
            dma((2, m // 2)),
            dma((2, m // 2)),
            dma((2, m // 2)),
            dma((2, m // 2)),
            dma((n,)),
            dma((n,)),
            dma((m,)),
            dma((m,)),
        ],
        compiler_params=pltpu.CompilerParams(
            collective_id=0, has_side_effects=True, vmem_limit_bytes=VMEM_BYTES
        ),
        name="gather_and_weigh",
    )(xa.T, xf.T, ca, cf, va, vf, live_hot, same)


def update_kernel(example_count, x_ref, c_ref, w_ref, m_ref, v_ref, w_out, m_out, v_out):
    scaled = x_ref[...]
    for j in range(w_ref.shape[1] // TILE):
        cols = slice(j * TILE, (j + 1) * TILE)
        gradient = lax.dot_general(
            scaled, c_ref[0, cols, :], (((1,), (1,)), ((), ())),
            preferred_element_type=jnp.float32,
        ) * (1.0 / example_count)
        moment_new = first_decay * m_ref[:, cols].astype(jnp.float32) + (1.0 - first_decay) * gradient
        second_new = (
            second_decay * v_ref[:, cols].astype(jnp.float32)
            + (1.0 - second_decay) * (gradient * gradient)
        )
        unbiased = second_new * (1.0 / second_bias)
        root = unbiased * lax.rsqrt(unbiased)
        step_dir = moment_new * (1.0 / first_bias) * refined_reciprocal(root + epsilon)
        weight = w_ref[:, cols].astype(jnp.float32)
        updated = (1.0 - learn_rate * weight_decay) * weight - learn_rate * step_dir
        w_out[:, cols] = updated.astype(jnp.bfloat16)
        m_out[:, cols] = moment_new.astype(jnp.bfloat16)
        v_out[:, cols] = second_new.astype(jnp.bfloat16)


def update(layer, example_count, scaled, cotangents, weight, moment, second):
    rows, columns = weight.shape
    tokens = scaled.shape[1]
    state = pl.BlockSpec((TILE, columns), lambda i: (i, 0))
    shape = jax.ShapeDtypeStruct((rows, columns), jnp.bfloat16)
    return pl.pallas_call(
        functools.partial(update_kernel, example_count),
        grid=(rows // TILE,),
        in_specs=[
            pl.BlockSpec((TILE, tokens), lambda i: (i, 0)),
            pl.BlockSpec((1, columns, tokens), lambda i: (layer, 0, 0)),
            state,
            state,
            state,
        ],
        out_specs=(state, state, state),
        out_shape=(shape, shape, shape),
        compiler_params=pltpu.CompilerParams(vmem_limit_bytes=VMEM_BYTES),
        name="update",
    )(scaled, cotangents, weight, moment, second)


def per_device_kernels(
    n, m,
    attention_input,
    feedforward_input,
    attention_cotangent,
    feedforward_cotangent,
    lengths,
    groups,
    attention_weight,
    attention_moment,
    attention_second,
    feedforward_weight,
    feedforward_moment,
    feedforward_second,
):
    example_count = lengths.shape[0]
    xa, xf, gathered = gather_and_weigh(
        n, m, attention_input, feedforward_input, attention_cotangent, feedforward_cotangent,
        attention_second, feedforward_second, lengths, groups,
    )
    gathered = gathered.reshape(2, -1, gathered.shape[3])
    attention_new = update(
        0, example_count, xa, gathered, attention_weight, attention_moment, attention_second
    )
    feedforward_new = update(
        1, example_count, xf, gathered, feedforward_weight, feedforward_moment, feedforward_second
    )
    return attention_new + feedforward_new


def fits_kernels(n, m, xa, xf, ca, lengths):
    examples = lengths.shape[0]
    tokens = ca.shape[1]
    return (
        n % 2 == 0
        and n >= 6
        and m % 2 == 0
        and examples <= ROWS_PAD
        and tokens % GROUP == 0
        and GROUP % (tokens // examples) == 0
        and ca.shape[0] // (n * m) == TILE
        and xa.shape[0] // n % TILE == 0
        and xf.shape[0] // n % TILE == 0
        and tokens // m % 16 == 0
    )


def solution(mesh):
    n, m = mesh.shape["fsdp"], mesh.shape["dp"]

    def step(*arrays):
        xa, xf, ca, _, lengths = arrays[:5]
        if fits_kernels(n, m, xa, xf, ca, lengths):
            return sharded(mesh, functools.partial(per_device_kernels, n, m))(*arrays)
        return sharded(mesh, per_device)(*arrays)

    return step


def sharded(mesh, body):
    return jax.shard_map(
        body,
        mesh=mesh,
        in_specs=(
            P("fsdp", "dp"),
            P("fsdp", "dp"),
            P(("dp", "fsdp"), None),
            P(("dp", "fsdp"), None),
            P(),
            P(),
            P("fsdp", "dp"),
            P("fsdp", "dp"),
            P("fsdp", "dp"),
            P("fsdp", "dp"),
            P("fsdp", "dp"),
            P("fsdp", "dp"),
        ),
        out_specs=(
            P("fsdp", "dp"),
            P("fsdp", "dp"),
            P("fsdp", "dp"),
            P("fsdp", "dp"),
            P("fsdp", "dp"),
            P("fsdp", "dp"),
        ),
        check_vma=False,
    )
```

```python
import functools

import jax
import jax.numpy as jnp
from jax import lax
from jax.experimental import pallas as pl
from jax.experimental.pallas import tpu as pltpu
from jax.sharding import PartitionSpec as P

first_decay = 0.9
second_decay = 0.95
first_bias = 1.0 - 0.9**10
second_bias = 1.0 - 0.95**10
learn_rate = 0.01
weight_decay = 0.1
epsilon = 1e-08
norm_epsilon = 1e-06


def live_tokens(lengths, slot_len):
    position = lax.broadcasted_iota(jnp.int32, (lengths.shape[0], slot_len), 1)
    return (position < lengths[:, None]).reshape(-1)


def example_norms(inputs, cotangents, second, slot_len):
    precond = 1.0 / (jnp.sqrt(second.astype(jnp.float32)) + epsilon)
    example_count = inputs.shape[1] // slot_len

    def one_example(example, norm_vals):
        inputs_slot = lax.dynamic_slice_in_dim(inputs, example * slot_len, slot_len, 1)
        grads_slot = lax.dynamic_slice_in_dim(cotangents, example * slot_len, slot_len, 1)
        tile_block = lax.dot_general(
            inputs_slot, grads_slot, (((1,), (1,)), ((), ())), preferred_element_type=jnp.float32
        )
        return norm_vals.at[example].set(jnp.sum(tile_block * tile_block * precond))

    return lax.fori_loop(0, example_count, one_example, jnp.zeros((example_count,), jnp.float32))


def importance(norm_vals, groups):
    strength = jnp.sqrt(norm_vals + norm_epsilon)
    same_group = (groups[:, None] == groups[None, :]).astype(jnp.float32)
    group_total = jnp.sum(same_group * strength[None, :], axis=1)
    group_count = jnp.sum(same_group, axis=1)
    return group_count * strength / group_total


def weighted_gradient(inputs, cotangents, token_weight, example_count):
    scaled = (inputs.astype(jnp.float32) * token_weight[None, :]).astype(jnp.bfloat16)
    product = lax.dot_general(
        scaled, cotangents, (((1,), (1,)), ((), ())), preferred_element_type=jnp.float32
    )
    return product / example_count


def adamw_step(weight, moment, second, gradient):
    moment_new = first_decay * moment.astype(jnp.float32) + (1.0 - first_decay) * gradient
    second_new = (
        second_decay * second.astype(jnp.float32) + (1.0 - second_decay) * gradient * gradient
    )
    step_dir = moment_new / first_bias / (jnp.sqrt(second_new / second_bias) + epsilon)
    weight_wide = weight.astype(jnp.float32)
    updated = weight_wide - learn_rate * (step_dir + weight_decay * weight_wide)
    return (
        updated.astype(jnp.bfloat16),
        moment_new.astype(jnp.bfloat16),
        second_new.astype(jnp.bfloat16),
    )


def per_device(
    attention_input,
    feedforward_input,
    attention_cotangent,
    feedforward_cotangent,
    lengths,
    groups,
    attention_weight,
    attention_moment,
    attention_second,
    feedforward_weight,
    feedforward_moment,
    feedforward_second,
):
    example_count = lengths.shape[0]
    attention_full, feedforward_full = (
        lax.all_gather(attention_input, "dp", axis=1, tiled=True),
        lax.all_gather(feedforward_input, "dp", axis=1, tiled=True),
    )
    slot_len = attention_full.shape[1] // example_count
    live_mask = live_tokens(lengths, slot_len)
    attention_live = jnp.where(live_mask[None, :], attention_full, jnp.zeros_like(attention_full))
    feedforward_live = jnp.where(
        live_mask[None, :], feedforward_full, jnp.zeros_like(feedforward_full)
    )
    attention_columns, feedforward_columns = (
        lax.all_gather(attention_cotangent, "fsdp", axis=0, tiled=True),
        lax.all_gather(feedforward_cotangent, "fsdp", axis=0, tiled=True),
    )
    attention_part = example_norms(attention_live, attention_columns, attention_second, slot_len)
    feedforward_part = example_norms(
        feedforward_live, feedforward_columns, feedforward_second, slot_len
    )
    norm_vals = lax.psum(attention_part + feedforward_part, ("dp", "fsdp"))
    weights = importance(norm_vals, groups)
    token_weight = jnp.repeat(weights, slot_len) * live_mask.astype(jnp.float32)
    attention_grad = weighted_gradient(
        attention_live, attention_columns, token_weight, example_count
    )
    feedforward_grad = weighted_gradient(
        feedforward_live, feedforward_columns, token_weight, example_count
    )
    attention_new = adamw_step(attention_weight, attention_moment, attention_second, attention_grad)
    feedforward_new = adamw_step(
        feedforward_weight, feedforward_moment, feedforward_second, feedforward_grad
    )
    return (
        attention_new[0],
        attention_new[1],
        attention_new[2],
        feedforward_new[0],
        feedforward_new[1],
        feedforward_new[2],
    )


MESH = pl.DeviceIdType.MESH
TILE = 256
GROUP = 128
ROWS_PAD = 16
VMEM_BYTES = 56 * 2**20


def inverse_root(value):
    guess = lax.rsqrt(value)
    return guess * (2.0 - (value * guess + epsilon) * guess)


def gather_kernel(
    n, m, slot_len, example_count,
    xa_in, xf_in, ca_in, cf_in, va_in, vf_in, live_ref, same_ref,
    xa_out, xf_out, c_out,
    xa_t, xf_t, x_rows, cbuf, ct, picked, vbuf, acc, norm_f, norm_d,
    local_sem, out_sem, c_send, c_recv, x_send, x_recv, core_send, core_recv,
    f_send, f_recv, d_send, d_recv,
):
    me_d, me_f = lax.axis_index("dp"), lax.axis_index("fsdp")
    position = lax.select(lax.rem(me_f, 2) == 0, me_f // 2, n - 1 - me_f // 2)

    def ring_index(place):
        place = lax.rem(place + n, n)
        return lax.select(place < n // 2, 2 * place, 2 * (n - 1 - place) + 1)

    rows_a, rows_f = xa_in.shape[1], xf_in.shape[1]
    share, block = xa_in.shape[0], ca_in.shape[0]
    tiles_a, tiles_f = rows_a // TILE, rows_f // TILE
    groups = live_ref.shape[1] // GROUP
    per_group = GROUP // slot_len
    high, core, m_high = me_d // 2, lax.rem(me_d, 2), m // 2

    x_bufs = (xa_t, xf_t)

    def x_slot(layer, owner):
        return x_bufs[layer].at[pl.ds(pl.multiple_of(owner * share, 16), share)]

    own = []
    for index, (src, dst) in enumerate((
        (ca_in, cbuf.at[0, me_f]),
        (cf_in, cbuf.at[1, me_f]),
        (xa_in, x_slot(0, me_d)),
        (xf_in, x_slot(1, me_d)),
        (va_in, vbuf.at[pl.ds(0, rows_a)]),
        (vf_in, vbuf.at[pl.ds(rows_a, rows_f)]),
    )):
        copy = pltpu.make_async_copy(src, dst, local_sem.at[index])
        copy.start()
        own.append(copy)

    barrier = pltpu.get_barrier_semaphore()
    for k in range(1, n):
        pl.semaphore_signal(
            barrier, inc=1, device_id={"fsdp": lax.rem(me_f + k, n)}, device_id_type=MESH
        )
    for k in range(1, m):
        pl.semaphore_signal(
            barrier, inc=1, device_id={"dp": lax.rem(me_d + k, m)}, device_id_type=MESH
        )
    pl.semaphore_wait(barrier, n + m - 2)

    def c_copy(layer, way, step):
        sign = 1 - 2 * way
        slot = cbuf.at[layer, ring_index(position - sign * step)]
        return pltpu.make_async_remote_copy(
            src_ref=slot, dst_ref=slot,
            send_sem=c_send.at[layer, way, step], recv_sem=c_recv.at[layer, way, step],
            device_id={"fsdp": ring_index(position + sign)}, device_id_type=MESH,
        )

    def x_copy(layer, k):
        slot = x_slot(layer, me_d)
        return pltpu.make_async_remote_copy(
            src_ref=slot, dst_ref=slot,
            send_sem=x_send.at[layer, k], recv_sem=x_recv.at[layer, k],
            device_id={"dp": lax.rem(high + k, m_high) * 2 + core}, device_id_type=MESH,
        )

    def core_copy(layer, k):
        slot = x_slot(layer, lax.rem(high + m_high - k, m_high) * 2 + core)
        return pltpu.make_async_remote_copy(
            src_ref=slot, dst_ref=slot,
            send_sem=core_send.at[layer, k], recv_sem=core_recv.at[layer, k],
            device_id={"dp": high * 2 + 1 - core}, device_id_type=MESH,
        )

    pairs = [(layer, way) for layer in range(2) for way in range(2)]
    last = n // 2 - 1

    def c_pairs(step):
        return pairs if step < last else [(0, 0), (1, 1)]

    for layer in range(2):
        own[layer].wait()
        for way in range(2):
            c_copy(layer, way, 0).start()
    for layer in range(2):
        own[2 + layer].wait()
        for k in range(1, m_high):
            x_copy(layer, k).start()
        core_copy(layer, 0).start()
    acc[...] = jnp.zeros_like(acc)
    picked[...] = jnp.zeros_like(picked)
    alive = jnp.sum(live_ref[...], axis=0, keepdims=True).astype(jnp.bfloat16)

    def advance(step):
        for layer, way in c_pairs(step):
            c_copy(layer, way, step).wait_recv()
            if (layer, way) in (c_pairs(step + 1) if step < last else []):
                c_copy(layer, way, step + 1).start()

    def take_inputs(layer):
        for k in range(1, m_high):
            x_copy(layer, k).wait_recv()
            core_copy(layer, k).start()
        for k in range(m_high):
            core_copy(layer, k).wait_recv()
        buf, base, tiles = x_bufs[layer], (0, rows_a)[layer], (tiles_a, tiles_f)[layer]

        def turn(tile, carry):
            here = pl.multiple_of(tile * TILE, TILE)
            there = pl.multiple_of(base + tile * TILE, TILE)
            for g in range(groups):
                x_rows[g, pl.ds(there, TILE), :] = buf[
                    pl.ds(g * GROUP, GROUP), pl.ds(here, TILE)
                ].T
            return carry

        lax.fori_loop(0, tiles, turn, 0)

    def unit(layer, owner):
        column = pl.multiple_of(owner * block, 128)
        tile_from, tile_to = ((0, tiles_a), (tiles_a, tiles_a + tiles_f))[layer]
        for g in range(groups):
            lanes = slice(g * GROUP, (g + 1) * GROUP)
            turned = (cbuf[layer, owner, :, pl.ds(g * GROUP, GROUP)] * alive[:, lanes]).T
            ct[layer, pl.ds(g * GROUP, GROUP), pl.ds(column, block)] = turned
            for q in range(per_group):
                rows = slice(q * slot_len, (q + 1) * slot_len)
                picked[g * per_group + q, rows, :] = turned[rows]

        def one_tile(tile, carry):
            row = pl.multiple_of(tile * TILE, TILE)
            second = vbuf[pl.ds(row, TILE), pl.ds(column, block)].astype(jnp.float32)
            precond = inverse_root(second)
            for e in range(example_count):
                product = jnp.dot(
                    x_rows[e // per_group, pl.ds(row, TILE), :], picked[e],
                    preferred_element_type=jnp.float32,
                )
                square = product * product * precond
                acc[e] += jnp.sum(square.reshape(TILE // 8, 8, block), axis=0)
            return carry

        lax.fori_loop(tile_from, tile_to, one_tile, 0)

    def both_ways(layers, step):
        def one_way(way, carry):
            for layer in layers:
                unit(layer, ring_index(position - (1 - 2 * way) * (step + 1)))
            return carry

        lax.fori_loop(0, 2, one_way, 0)

    own[4].wait()
    own[5].wait()
    take_inputs(0)
    unit(0, me_f)
    advance(0)
    both_ways((0,), 0)
    take_inputs(1)
    unit(1, me_f)
    advance(1)
    both_ways((1,), 0)
    for step in range(2, last + 1):
        advance(step)
        both_ways((0, 1), step - 1)
    for layer in range(2):
        unit(layer, ring_index(position + n // 2))

    c_store = pltpu.make_async_copy(ct, c_out, out_sem)
    c_store.start()

    partial = jnp.sum(jnp.sum(acc[...], axis=1), axis=1, keepdims=True)
    norm_f[me_f] = jnp.broadcast_to(partial, (ROWS_PAD, 128))

    def sum_over(axis, count, me, buf, send, recv):
        copies = []
        for k in range(1, count):
            copy = pltpu.make_async_remote_copy(
                src_ref=buf.at[me], dst_ref=buf.at[me],
                send_sem=send.at[k], recv_sem=recv.at[k],
                device_id={axis: lax.rem(me + k, count)}, device_id_type=MESH,
            )
            copy.start()
            copies.append(copy)
        for copy in copies:
            copy.wait_recv()
        return copies, jnp.sum(buf[...], axis=0)

    f_copies, over_f = sum_over("fsdp", n, me_f, norm_f, f_send, f_recv)
    norm_d[me_d] = over_f
    d_copies, norm_vals = sum_over("dp", m, me_d, norm_d, d_send, d_recv)

    strength = jnp.sqrt(norm_vals + norm_epsilon)
    same = same_ref[...]
    sub = lax.broadcasted_iota(jnp.int32, (ROWS_PAD, 128), 0)
    lane = lax.broadcasted_iota(jnp.int32, (ROWS_PAD, 128), 1)
    strength_row = jnp.sum(jnp.where(sub == lane, strength, 0.0), axis=0, keepdims=True)
    group_total = jnp.sum(same * strength_row, axis=1, keepdims=True)
    group_count = jnp.sum(same, axis=1, keepdims=True)
    weights = group_count * strength[:, :1] / group_total
    token_weight = jnp.sum(live_ref[...] * weights, axis=0, keepdims=True)

    for layer, out in ((0, xa_out), (1, xf_out)):
        base, tiles = (0, rows_a)[layer], (tiles_a, tiles_f)[layer]

        def scale(tile, carry, out=out, base=base):
            here = pl.multiple_of(tile * TILE, TILE)
            there = pl.multiple_of(base + tile * TILE, TILE)
            for g in range(groups):
                lanes = slice(g * GROUP, (g + 1) * GROUP)
                wide = x_rows[g, pl.ds(there, TILE), :].astype(jnp.float32)
                out[pl.ds(here, TILE), lanes] = (wide * token_weight[:, lanes]).astype(jnp.bfloat16)
            return carry

        lax.fori_loop(0, tiles, scale, 0)

    for step in range(last + 1):
        for layer, way in c_pairs(step):
            c_copy(layer, way, step).wait_send()
    for layer in range(2):
        for k in range(1, m_high):
            x_copy(layer, k).wait_send()
        for k in range(m_high):
            core_copy(layer, k).wait_send()
    for copy in f_copies + d_copies:
        copy.wait_send()
    c_store.wait()


def gather_and_weigh(n, m, xa, xf, ca, cf, va, vf, lengths, groups):
    example_count = lengths.shape[0]
    tokens = ca.shape[1]
    slot_len = tokens // example_count
    live = live_tokens(lengths, slot_len)
    example_of = jnp.arange(tokens, dtype=jnp.int32) // slot_len
    row = jnp.arange(ROWS_PAD, dtype=jnp.int32)
    live_hot = ((row[:, None] == example_of[None, :]) & live[None, :]).astype(jnp.float32)
    padded = jnp.concatenate([groups, -1 - jnp.arange(128 - example_count, dtype=jnp.int32)])
    same = (padded[:ROWS_PAD, None] == padded[None, :]).astype(jnp.float32)
    rows_a, rows_f, block = xa.shape[0], xf.shape[0], ca.shape[0]
    columns = n * block
    bf16, f32 = jnp.bfloat16, jnp.float32
    hbm = pl.BlockSpec(memory_space=pl.ANY)
    vmem = pl.BlockSpec(memory_space=pltpu.VMEM)
    dma = pltpu.SemaphoreType.DMA
    return pl.pallas_call(
        functools.partial(gather_kernel, n, m, slot_len, example_count),
        out_shape=(
            jax.ShapeDtypeStruct((rows_a, tokens), bf16),
            jax.ShapeDtypeStruct((rows_f, tokens), bf16),
            jax.ShapeDtypeStruct((2, tokens, columns), bf16),
        ),
        in_specs=[hbm] * 6 + [vmem] * 2,
        out_specs=(vmem, vmem, hbm),
        scratch_shapes=[
            pltpu.VMEM((tokens, rows_a), bf16),
            pltpu.VMEM((tokens, rows_f), bf16),
            pltpu.VMEM((tokens // GROUP, rows_a + rows_f, GROUP), bf16),
            pltpu.VMEM((2, n, block, tokens), bf16),
            pltpu.VMEM((2, tokens, columns), bf16),
            pltpu.VMEM((example_count, GROUP, block), bf16),
            pltpu.VMEM((rows_a + rows_f, columns), bf16),
            pltpu.VMEM((ROWS_PAD, 8, block), f32),
            pltpu.VMEM((n, ROWS_PAD, 128), f32),
            pltpu.VMEM((m, ROWS_PAD, 128), f32),
            dma((6,)),
            dma,
            dma((2, 2, n // 2)),
            dma((2, 2, n // 2)),
            dma((2, m // 2)),
            dma((2, m // 2)),
            dma((2, m // 2)),
            dma((2, m // 2)),
            dma((n,)),
            dma((n,)),
            dma((m,)),
            dma((m,)),
        ],
        compiler_params=pltpu.CompilerParams(
            collective_id=0, has_side_effects=True, vmem_limit_bytes=VMEM_BYTES
        ),
        name="gather_and_weigh",
    )(xa.T, xf.T, ca, cf, va, vf, live_hot, same)


def update_kernel(example_count, x_ref, c_ref, w_ref, m_ref, v_ref, w_out, m_out, v_out):
    scaled = x_ref[...]
    for j in range(w_ref.shape[1] // TILE):
        cols = slice(j * TILE, (j + 1) * TILE)
        product = jnp.dot(scaled, c_ref[0, :, cols], preferred_element_type=jnp.float32)
        moment_new = first_decay * m_ref[:, cols].astype(jnp.float32) + (
            (1.0 - first_decay) / example_count
        ) * product
        second_new = second_decay * v_ref[:, cols].astype(jnp.float32) + (
            (1.0 - second_decay) / example_count**2
        ) * (product * product)
        inverse = inverse_root(second_new * (1.0 / second_bias))
        weight = w_ref[:, cols].astype(jnp.float32)
        updated = (1.0 - learn_rate * weight_decay) * weight - (
            (learn_rate / first_bias) * moment_new
        ) * inverse
        w_out[:, cols] = updated.astype(jnp.bfloat16)
        m_out[:, cols] = moment_new.astype(jnp.bfloat16)
        v_out[:, cols] = second_new.astype(jnp.bfloat16)


def update(layer, example_count, scaled, cotangents, weight, moment, second):
    rows, columns = weight.shape
    tokens = scaled.shape[1]
    state = pl.BlockSpec((TILE, columns), lambda i: (i, 0))
    shape = jax.ShapeDtypeStruct((rows, columns), jnp.bfloat16)
    return pl.pallas_call(
        functools.partial(update_kernel, example_count),
        grid=(rows // TILE,),
        in_specs=[
            pl.BlockSpec((TILE, tokens), lambda i: (i, 0)),
            pl.BlockSpec((1, tokens, columns), lambda i: (layer, 0, 0)),
            state,
            state,
            state,
        ],
        out_specs=(state, state, state),
        out_shape=(shape, shape, shape),
        compiler_params=pltpu.CompilerParams(vmem_limit_bytes=VMEM_BYTES),
        name="update",
    )(scaled, cotangents, weight, moment, second)


def per_device_kernels(
    n, m,
    attention_input,
    feedforward_input,
    attention_cotangent,
    feedforward_cotangent,
    lengths,
    groups,
    attention_weight,
    attention_moment,
    attention_second,
    feedforward_weight,
    feedforward_moment,
    feedforward_second,
):
    example_count = lengths.shape[0]
    xa, xf, gathered = gather_and_weigh(
        n, m, attention_input, feedforward_input, attention_cotangent, feedforward_cotangent,
        attention_second, feedforward_second, lengths, groups,
    )
    attention_new = update(
        0, example_count, xa, gathered, attention_weight, attention_moment, attention_second
    )
    feedforward_new = update(
        1, example_count, xf, gathered, feedforward_weight, feedforward_moment, feedforward_second
    )
    return attention_new + feedforward_new


def fits_kernels(n, m, xa, xf, ca, lengths):
    examples = lengths.shape[0]
    tokens = ca.shape[1]
    return (
        n % 2 == 0
        and n >= 6
        and m % 2 == 0
        and examples <= ROWS_PAD
        and tokens % GROUP == 0
        and GROUP % (tokens // examples) == 0
        and (tokens // examples) % 16 == 0
        and ca.shape[0] // (n * m) == TILE
        and xa.shape[0] // n % TILE == 0
        and xf.shape[0] // n % TILE == 0
        and tokens // m % 16 == 0
    )


def solution(mesh):
    n, m = mesh.shape["fsdp"], mesh.shape["dp"]

    def step(*arrays):
        xa, xf, ca, _, lengths = arrays[:5]
        if fits_kernels(n, m, xa, xf, ca, lengths):
            return sharded(mesh, functools.partial(per_device_kernels, n, m))(*arrays)
        return sharded(mesh, per_device)(*arrays)

    return step


def sharded(mesh, body):
    return jax.shard_map(
        body,
        mesh=mesh,
        in_specs=(
            P("fsdp", "dp"),
            P("fsdp", "dp"),
            P(("dp", "fsdp"), None),
            P(("dp", "fsdp"), None),
            P(),
            P(),
            P("fsdp", "dp"),
            P("fsdp", "dp"),
            P("fsdp", "dp"),
            P("fsdp", "dp"),
            P("fsdp", "dp"),
            P("fsdp", "dp"),
        ),
        out_specs=(
            P("fsdp", "dp"),
            P("fsdp", "dp"),
            P("fsdp", "dp"),
            P("fsdp", "dp"),
            P("fsdp", "dp"),
            P("fsdp", "dp"),
        ),
        check_vma=False,
    )
```

```python
import functools

import jax
import jax.numpy as jnp
from jax import lax
from jax.experimental import pallas as pl
from jax.experimental.pallas import tpu as pltpu
from jax.sharding import PartitionSpec as P

first_decay = 0.9
second_decay = 0.95
first_bias = 1.0 - 0.9**10
second_bias = 1.0 - 0.95**10
learn_rate = 0.01
weight_decay = 0.1
epsilon = 1e-08
norm_epsilon = 1e-06


def live_tokens(lengths, slot_len):
    position = lax.broadcasted_iota(jnp.int32, (lengths.shape[0], slot_len), 1)
    return (position < lengths[:, None]).reshape(-1)


def example_norms(inputs, cotangents, second, slot_len):
    precond = 1.0 / (jnp.sqrt(second.astype(jnp.float32)) + epsilon)
    example_count = inputs.shape[1] // slot_len

    def one_example(example, norm_vals):
        inputs_slot = lax.dynamic_slice_in_dim(inputs, example * slot_len, slot_len, 1)
        grads_slot = lax.dynamic_slice_in_dim(cotangents, example * slot_len, slot_len, 1)
        tile_block = lax.dot_general(
            inputs_slot, grads_slot, (((1,), (1,)), ((), ())), preferred_element_type=jnp.float32
        )
        return norm_vals.at[example].set(jnp.sum(tile_block * tile_block * precond))

    return lax.fori_loop(0, example_count, one_example, jnp.zeros((example_count,), jnp.float32))


def importance(norm_vals, groups):
    strength = jnp.sqrt(norm_vals + norm_epsilon)
    same_group = (groups[:, None] == groups[None, :]).astype(jnp.float32)
    group_total = jnp.sum(same_group * strength[None, :], axis=1)
    group_count = jnp.sum(same_group, axis=1)
    return group_count * strength / group_total


def weighted_gradient(inputs, cotangents, token_weight, example_count):
    scaled = (inputs.astype(jnp.float32) * token_weight[None, :]).astype(jnp.bfloat16)
    product = lax.dot_general(
        scaled, cotangents, (((1,), (1,)), ((), ())), preferred_element_type=jnp.float32
    )
    return product / example_count


def adamw_step(weight, moment, second, gradient):
    moment_new = first_decay * moment.astype(jnp.float32) + (1.0 - first_decay) * gradient
    second_new = (
        second_decay * second.astype(jnp.float32) + (1.0 - second_decay) * gradient * gradient
    )
    step_dir = moment_new / first_bias / (jnp.sqrt(second_new / second_bias) + epsilon)
    weight_wide = weight.astype(jnp.float32)
    updated = weight_wide - learn_rate * (step_dir + weight_decay * weight_wide)
    return (
        updated.astype(jnp.bfloat16),
        moment_new.astype(jnp.bfloat16),
        second_new.astype(jnp.bfloat16),
    )


def per_device(
    attention_input,
    feedforward_input,
    attention_cotangent,
    feedforward_cotangent,
    lengths,
    groups,
    attention_weight,
    attention_moment,
    attention_second,
    feedforward_weight,
    feedforward_moment,
    feedforward_second,
):
    example_count = lengths.shape[0]
    attention_full, feedforward_full = (
        lax.all_gather(attention_input, "dp", axis=1, tiled=True),
        lax.all_gather(feedforward_input, "dp", axis=1, tiled=True),
    )
    slot_len = attention_full.shape[1] // example_count
    live_mask = live_tokens(lengths, slot_len)
    attention_live = jnp.where(live_mask[None, :], attention_full, jnp.zeros_like(attention_full))
    feedforward_live = jnp.where(
        live_mask[None, :], feedforward_full, jnp.zeros_like(feedforward_full)
    )
    attention_columns, feedforward_columns = (
        lax.all_gather(attention_cotangent, "fsdp", axis=0, tiled=True),
        lax.all_gather(feedforward_cotangent, "fsdp", axis=0, tiled=True),
    )
    attention_part = example_norms(attention_live, attention_columns, attention_second, slot_len)
    feedforward_part = example_norms(
        feedforward_live, feedforward_columns, feedforward_second, slot_len
    )
    norm_vals = lax.psum(attention_part + feedforward_part, ("dp", "fsdp"))
    weights = importance(norm_vals, groups)
    token_weight = jnp.repeat(weights, slot_len) * live_mask.astype(jnp.float32)
    attention_grad = weighted_gradient(
        attention_live, attention_columns, token_weight, example_count
    )
    feedforward_grad = weighted_gradient(
        feedforward_live, feedforward_columns, token_weight, example_count
    )
    attention_new = adamw_step(attention_weight, attention_moment, attention_second, attention_grad)
    feedforward_new = adamw_step(
        feedforward_weight, feedforward_moment, feedforward_second, feedforward_grad
    )
    return (
        attention_new[0],
        attention_new[1],
        attention_new[2],
        feedforward_new[0],
        feedforward_new[1],
        feedforward_new[2],
    )


MESH = pl.DeviceIdType.MESH
TILE = 256
GROUP = 128
ROWS_PAD = 16
VMEM_BYTES = 56 * 2**20


def inverse_root(value):
    guess = lax.rsqrt(value)
    return guess * (2.0 - (value * guess + epsilon) * guess)


def gather_kernel(
    n, m, slot_len, example_count,
    xa_in, xf_in, ca_in, cf_in, va_in, vf_in, lengths_ref, groups_ref,
    xa_out, xf_out, c_out,
    xa_t, xf_t, x_rows, cbuf, ct, picked, live_ref, vbuf, acc, norm_f, norm_d,
    local_sem, out_sem, c_send, c_recv, x_send, x_recv, core_send, core_recv,
    f_send, f_recv, d_send, d_recv,
):
    me_d, me_f = lax.axis_index("dp"), lax.axis_index("fsdp")
    position = lax.select(lax.rem(me_f, 2) == 0, me_f // 2, n - 1 - me_f // 2)

    def ring_index(place):
        place = lax.rem(place + n, n)
        return lax.select(place < n // 2, 2 * place, 2 * (n - 1 - place) + 1)

    rows_a, rows_f = xa_in.shape[1], xf_in.shape[1]
    share, block = xa_in.shape[0], ca_in.shape[0]
    tiles_a, tiles_f = rows_a // TILE, rows_f // TILE
    groups = live_ref.shape[1] // GROUP
    per_group = GROUP // slot_len
    high, core, m_high = me_d // 2, lax.rem(me_d, 2), m // 2

    x_bufs = (xa_t, xf_t)

    def x_slot(layer, owner):
        return x_bufs[layer].at[pl.ds(pl.multiple_of(owner * share, 16), share)]

    own = []
    for index, (src, dst) in enumerate((
        (ca_in, cbuf.at[0, me_f]),
        (cf_in, cbuf.at[1, me_f]),
        (xa_in, x_slot(0, me_d)),
        (xf_in, x_slot(1, me_d)),
        (va_in, vbuf.at[pl.ds(0, rows_a)]),
        (vf_in, vbuf.at[pl.ds(rows_a, rows_f)]),
    )):
        copy = pltpu.make_async_copy(src, dst, local_sem.at[index])
        copy.start()
        own.append(copy)

    barrier = pltpu.get_barrier_semaphore()
    for k in range(1, n):
        pl.semaphore_signal(
            barrier, inc=1, device_id={"fsdp": lax.rem(me_f + k, n)}, device_id_type=MESH
        )
    for k in range(1, m):
        pl.semaphore_signal(
            barrier, inc=1, device_id={"dp": lax.rem(me_d + k, m)}, device_id_type=MESH
        )
    pl.semaphore_wait(barrier, n + m - 2)

    def c_copy(layer, way, step):
        sign = 1 - 2 * way
        slot = cbuf.at[layer, ring_index(position - sign * step)]
        return pltpu.make_async_remote_copy(
            src_ref=slot, dst_ref=slot,
            send_sem=c_send.at[layer, way, step], recv_sem=c_recv.at[layer, way, step],
            device_id={"fsdp": ring_index(position + sign)}, device_id_type=MESH,
        )

    def x_copy(layer, k):
        slot = x_slot(layer, me_d)
        return pltpu.make_async_remote_copy(
            src_ref=slot, dst_ref=slot,
            send_sem=x_send.at[layer, k], recv_sem=x_recv.at[layer, k],
            device_id={"dp": lax.rem(high + k, m_high) * 2 + core}, device_id_type=MESH,
        )

    def core_copy(layer, k):
        slot = x_slot(layer, lax.rem(high + m_high - k, m_high) * 2 + core)
        return pltpu.make_async_remote_copy(
            src_ref=slot, dst_ref=slot,
            send_sem=core_send.at[layer, k], recv_sem=core_recv.at[layer, k],
            device_id={"dp": high * 2 + 1 - core}, device_id_type=MESH,
        )

    pairs = [(layer, way) for layer in range(2) for way in range(2)]
    last = n // 2 - 1

    def c_pairs(step):
        return pairs if step < last else [(0, 0), (1, 1)]

    for layer in range(2):
        own[layer].wait()
        for way in range(2):
            c_copy(layer, way, 0).start()
    for layer in range(2):
        own[2 + layer].wait()
        for k in range(1, m_high):
            x_copy(layer, k).start()
        core_copy(layer, 0).start()
    acc[...] = jnp.zeros_like(acc)
    picked[...] = jnp.zeros_like(picked)
    token = lax.broadcasted_iota(jnp.int32, (ROWS_PAD, live_ref.shape[1]), 1)
    token_row = lax.broadcasted_iota(jnp.int32, (ROWS_PAD, live_ref.shape[1]), 0)
    offset = token - token_row * slot_len
    limit = jnp.zeros_like(token)
    for e in range(example_count):
        limit = jnp.where(token_row == e, lengths_ref[e], limit)
    live_ref[...] = jnp.where(
        (offset >= 0) & (offset < jnp.minimum(limit, slot_len)), 1.0, 0.0
    ).astype(jnp.float32)
    alive = jnp.sum(live_ref[...], axis=0, keepdims=True).astype(jnp.bfloat16)

    def advance(step):
        for layer, way in c_pairs(step):
            c_copy(layer, way, step).wait_recv()
            if (layer, way) in (c_pairs(step + 1) if step < last else []):
                c_copy(layer, way, step + 1).start()

    def take_inputs(layer):
        for k in range(1, m_high):
            x_copy(layer, k).wait_recv()
            core_copy(layer, k).start()
        for k in range(m_high):
            core_copy(layer, k).wait_recv()
        buf, base, tiles = x_bufs[layer], (0, rows_a)[layer], (tiles_a, tiles_f)[layer]

        def turn(tile, carry):
            here = pl.multiple_of(tile * TILE, TILE)
            there = pl.multiple_of(base + tile * TILE, TILE)
            for g in range(groups):
                x_rows[g, pl.ds(there, TILE), :] = buf[
                    pl.ds(g * GROUP, GROUP), pl.ds(here, TILE)
                ].T
            return carry

        lax.fori_loop(0, tiles, turn, 0)

    def unit(layer, owner):
        column = pl.multiple_of(owner * block, 128)
        tile_from, tile_to = ((0, tiles_a), (tiles_a, tiles_a + tiles_f))[layer]
        for g in range(groups):
            lanes = slice(g * GROUP, (g + 1) * GROUP)
            turned = (cbuf[layer, owner, :, pl.ds(g * GROUP, GROUP)] * alive[:, lanes]).T
            ct[layer, pl.ds(g * GROUP, GROUP), pl.ds(column, block)] = turned
            for q in range(per_group):
                rows = slice(q * slot_len, (q + 1) * slot_len)
                picked[g * per_group + q, rows, :] = turned[rows]

        def one_tile(tile, carry):
            row = pl.multiple_of(tile * TILE, TILE)
            second = vbuf[pl.ds(row, TILE), pl.ds(column, block)].astype(jnp.float32)
            precond = inverse_root(second)
            for e in range(example_count):
                product = jnp.dot(
                    x_rows[e // per_group, pl.ds(row, TILE), :], picked[e],
                    preferred_element_type=jnp.float32,
                )
                square = product * product * precond
                acc[e] += jnp.sum(square.reshape(TILE // 8, 8, block), axis=0)
            return carry

        lax.fori_loop(tile_from, tile_to, one_tile, 0)

    def both_ways(layers, step):
        def one_way(way, carry):
            for layer in layers:
                unit(layer, ring_index(position - (1 - 2 * way) * (step + 1)))
            return carry

        lax.fori_loop(0, 2, one_way, 0)

    def one_side(way, step):
        for layer in range(2):
            unit(layer, ring_index(position - (1 - 2 * way) * (step + 1)))

    own[4].wait()
    own[5].wait()
    take_inputs(0)
    unit(0, me_f)
    advance(0)
    both_ways((0,), 0)
    take_inputs(1)
    unit(1, me_f)
    advance(1)
    both_ways((1,), 0)
    for step in range(2, last + 1):
        one_side(0, step - 1)
        advance(step)
        one_side(1, step - 1)
    for layer in range(2):
        unit(layer, ring_index(position + n // 2))

    c_store = pltpu.make_async_copy(ct, c_out, out_sem)
    c_store.start()

    partial = jnp.sum(jnp.sum(acc[...], axis=1), axis=1, keepdims=True)
    norm_f[me_f] = jnp.broadcast_to(partial, (ROWS_PAD, 128))

    def sum_over(axis, count, me, buf, send, recv):
        copies = []
        for k in range(1, count):
            copy = pltpu.make_async_remote_copy(
                src_ref=buf.at[me], dst_ref=buf.at[me],
                send_sem=send.at[k], recv_sem=recv.at[k],
                device_id={axis: lax.rem(me + k, count)}, device_id_type=MESH,
            )
            copy.start()
            copies.append(copy)
        for copy in copies:
            copy.wait_recv()
        return copies, jnp.sum(buf[...], axis=0)

    f_copies, over_f = sum_over("fsdp", n, me_f, norm_f, f_send, f_recv)
    norm_d[me_d] = over_f
    d_copies, norm_vals = sum_over("dp", m, me_d, norm_d, d_send, d_recv)

    strength = jnp.sqrt(norm_vals + norm_epsilon)
    sub = lax.broadcasted_iota(jnp.int32, (ROWS_PAD, 128), 0)
    lane = lax.broadcasted_iota(jnp.int32, (ROWS_PAD, 128), 1)
    row_group, lane_group = -1 - sub, -1 - lane
    for e in range(example_count):
        row_group = jnp.where(sub == e, groups_ref[e], row_group)
        lane_group = jnp.where(lane == e, groups_ref[e], lane_group)
    same = jnp.where(row_group == lane_group, 1.0, 0.0).astype(jnp.float32)
    strength_row = jnp.sum(jnp.where(sub == lane, strength, 0.0), axis=0, keepdims=True)
    group_total = jnp.sum(same * strength_row, axis=1, keepdims=True)
    group_count = jnp.sum(same, axis=1, keepdims=True)
    weights = group_count * strength[:, :1] / group_total
    token_weight = jnp.sum(live_ref[...] * weights, axis=0, keepdims=True)

    for layer, out in ((0, xa_out), (1, xf_out)):
        base, tiles = (0, rows_a)[layer], (tiles_a, tiles_f)[layer]

        def scale(tile, carry, out=out, base=base):
            here = pl.multiple_of(tile * TILE, TILE)
            there = pl.multiple_of(base + tile * TILE, TILE)
            for g in range(groups):
                lanes = slice(g * GROUP, (g + 1) * GROUP)
                wide = x_rows[g, pl.ds(there, TILE), :].astype(jnp.float32)
                out[pl.ds(here, TILE), lanes] = (wide * token_weight[:, lanes]).astype(jnp.bfloat16)
            return carry

        lax.fori_loop(0, tiles, scale, 0)

    for step in range(last + 1):
        for layer, way in c_pairs(step):
            c_copy(layer, way, step).wait_send()
    for layer in range(2):
        for k in range(1, m_high):
            x_copy(layer, k).wait_send()
        for k in range(m_high):
            core_copy(layer, k).wait_send()
    for copy in f_copies + d_copies:
        copy.wait_send()
    c_store.wait()


def gather_and_weigh(n, m, xa, xf, ca, cf, va, vf, lengths, groups):
    example_count = lengths.shape[0]
    tokens = ca.shape[1]
    slot_len = tokens // example_count
    rows_a, rows_f, block = xa.shape[0], xf.shape[0], ca.shape[0]
    columns = n * block
    bf16, f32 = jnp.bfloat16, jnp.float32
    hbm = pl.BlockSpec(memory_space=pl.ANY)
    vmem = pl.BlockSpec(memory_space=pltpu.VMEM)
    dma = pltpu.SemaphoreType.DMA
    return pl.pallas_call(
        functools.partial(gather_kernel, n, m, slot_len, example_count),
        out_shape=(
            jax.ShapeDtypeStruct((rows_a, tokens), bf16),
            jax.ShapeDtypeStruct((rows_f, tokens), bf16),
            jax.ShapeDtypeStruct((2, tokens, columns), bf16),
        ),
        in_specs=[hbm] * 6 + [pl.BlockSpec(memory_space=pltpu.SMEM)] * 2,
        out_specs=(vmem, vmem, hbm),
        scratch_shapes=[
            pltpu.VMEM((tokens, rows_a), bf16),
            pltpu.VMEM((tokens, rows_f), bf16),
            pltpu.VMEM((tokens // GROUP, rows_a + rows_f, GROUP), bf16),
            pltpu.VMEM((2, n, block, tokens), bf16),
            pltpu.VMEM((2, tokens, columns), bf16),
            pltpu.VMEM((example_count, GROUP, block), bf16),
            pltpu.VMEM((ROWS_PAD, tokens), f32),
            pltpu.VMEM((rows_a + rows_f, columns), bf16),
            pltpu.VMEM((ROWS_PAD, 8, block), f32),
            pltpu.VMEM((n, ROWS_PAD, 128), f32),
            pltpu.VMEM((m, ROWS_PAD, 128), f32),
            dma((6,)),
            dma,
            dma((2, 2, n // 2)),
            dma((2, 2, n // 2)),
            dma((2, m // 2)),
            dma((2, m // 2)),
            dma((2, m // 2)),
            dma((2, m // 2)),
            dma((n,)),
            dma((n,)),
            dma((m,)),
            dma((m,)),
        ],
        compiler_params=pltpu.CompilerParams(
            collective_id=0, has_side_effects=True, vmem_limit_bytes=VMEM_BYTES
        ),
        name="gather_and_weigh",
    )(xa.T, xf.T, ca, cf, va, vf, lengths, groups)


def update_kernel(example_count, x_ref, c_ref, w_ref, m_ref, v_ref, w_out, m_out, v_out):
    scaled = x_ref[...]
    for j in range(w_ref.shape[1] // TILE):
        cols = slice(j * TILE, (j + 1) * TILE)
        product = jnp.dot(scaled, c_ref[0, :, cols], preferred_element_type=jnp.float32)
        moment_new = first_decay * m_ref[:, cols].astype(jnp.float32) + (
            (1.0 - first_decay) / example_count
        ) * product
        second_new = second_decay * v_ref[:, cols].astype(jnp.float32) + (
            (1.0 - second_decay) / example_count**2
        ) * (product * product)
        inverse = inverse_root(second_new * (1.0 / second_bias))
        weight = w_ref[:, cols].astype(jnp.float32)
        updated = (1.0 - learn_rate * weight_decay) * weight - (
            (learn_rate / first_bias) * moment_new
        ) * inverse
        w_out[:, cols] = updated.astype(jnp.bfloat16)
        m_out[:, cols] = moment_new.astype(jnp.bfloat16)
        v_out[:, cols] = second_new.astype(jnp.bfloat16)


def update(layer, example_count, scaled, cotangents, weight, moment, second):
    rows, columns = weight.shape
    tokens = scaled.shape[1]
    state = pl.BlockSpec((TILE, columns), lambda i: (i, 0))
    shape = jax.ShapeDtypeStruct((rows, columns), jnp.bfloat16)
    return pl.pallas_call(
        functools.partial(update_kernel, example_count),
        grid=(rows // TILE,),
        in_specs=[
            pl.BlockSpec((TILE, tokens), lambda i: (i, 0)),
            pl.BlockSpec((1, tokens, columns), lambda i: (layer, 0, 0)),
            state,
            state,
            state,
        ],
        out_specs=(state, state, state),
        out_shape=(shape, shape, shape),
        compiler_params=pltpu.CompilerParams(vmem_limit_bytes=VMEM_BYTES),
        name="update",
    )(scaled, cotangents, weight, moment, second)


def per_device_kernels(
    n, m,
    attention_input,
    feedforward_input,
    attention_cotangent,
    feedforward_cotangent,
    lengths,
    groups,
    attention_weight,
    attention_moment,
    attention_second,
    feedforward_weight,
    feedforward_moment,
    feedforward_second,
):
    example_count = lengths.shape[0]
    xa, xf, gathered = gather_and_weigh(
        n, m, attention_input, feedforward_input, attention_cotangent, feedforward_cotangent,
        attention_second, feedforward_second, lengths, groups,
    )
    attention_new = update(
        0, example_count, xa, gathered, attention_weight, attention_moment, attention_second
    )
    feedforward_new = update(
        1, example_count, xf, gathered, feedforward_weight, feedforward_moment, feedforward_second
    )
    return attention_new + feedforward_new


def fits_kernels(n, m, xa, xf, ca, lengths):
    examples = lengths.shape[0]
    tokens = ca.shape[1]
    return (
        n % 2 == 0
        and n >= 6
        and m % 2 == 0
        and examples <= ROWS_PAD
        and tokens % GROUP == 0
        and GROUP % (tokens // examples) == 0
        and (tokens // examples) % 16 == 0
        and ca.shape[0] // (n * m) == TILE
        and xa.shape[0] // n % TILE == 0
        and xf.shape[0] // n % TILE == 0
        and tokens // m % 16 == 0
    )


def solution(mesh):
    n, m = mesh.shape["fsdp"], mesh.shape["dp"]

    def step(*arrays):
        xa, xf, ca, _, lengths = arrays[:5]
        if fits_kernels(n, m, xa, xf, ca, lengths):
            return sharded(mesh, functools.partial(per_device_kernels, n, m))(*arrays)
        return sharded(mesh, per_device)(*arrays)

    return step


def sharded(mesh, body):
    return jax.shard_map(
        body,
        mesh=mesh,
        in_specs=(
            P("fsdp", "dp"),
            P("fsdp", "dp"),
            P(("dp", "fsdp"), None),
            P(("dp", "fsdp"), None),
            P(),
            P(),
            P("fsdp", "dp"),
            P("fsdp", "dp"),
            P("fsdp", "dp"),
            P("fsdp", "dp"),
            P("fsdp", "dp"),
            P("fsdp", "dp"),
        ),
        out_specs=(
            P("fsdp", "dp"),
            P("fsdp", "dp"),
            P("fsdp", "dp"),
            P("fsdp", "dp"),
            P("fsdp", "dp"),
            P("fsdp", "dp"),
        ),
        check_vma=False,
    )
```
